256 devices in a mesh: ctx: 32 (over z, x_hi, core), head: 8 (over y, x_lo).
Axes of the slice: x: 4 (x_hi: 2, x_lo: 2; x = x_hi * 2 + x_lo), y: 4, z: 8, core: 2. Of those that a mesh axis runs over, the one named last changes fastest.
Arguments:
- query: bfloat16 [2, 16384, 4096], P(None, 'ctx', 'head'), may hold values from -12 to 12
- key_in: bfloat16 [2, 16384, 4096], P(None, 'ctx', 'head'), may hold values from -12 to 12
- value: bfloat16 [2, 16384, 4096], P(None, 'ctx', 'head'), may hold values from -6 to 6
- rates: float32 [2, 8, 16384], P(None, 'head', 'ctx'), may hold values from 0.03 to 0.3
- w_in: bfloat16 [8, 512, 512], P('head'), may hold values from -50 to 50
- w_gate: bfloat16 [8, 512, 512], P('head'), may hold values from -50 to 50
- w_out: bfloat16 [8, 512, 512], P('head'), may hold values from -50 to 50
- norm_gain: float32 [8, 512], P('head'), may hold values from 0.1 to 1.9
- proj_weight: bfloat16 [4096, 5120], P('head'), may hold values from -0.125 to 0.125
Outputs:
- mixed: bfloat16 [2, 16384, 5120], P(None, 'ctx', 'head')
- new_in: bfloat16 [8, 512, 512], P('head')
- new_gate: bfloat16 [8, 512, 512], P('head')
- new_out: bfloat16 [8, 512, 512], P('head')
The draws below stay inside these ranges and needn't reach their ends.
All inputs are finite; a program needn't handle non-finite values.
Results may differ from the reference program's by a relative error of at most 0.015.
Values may be sent and summed in bfloat16 or wider, within the bound.
A program may use at most 128 MiB of HBM per device.

```python
import math
import jax
import jax.numpy as jnp
from jax import lax

DH = 512
HID = 512
MODEL = 5120
HEADS = 8
TOKENS = 16384
GROUPS = 2
WINDOW = 1024


def paired_draw(key):
    shape_all = (GROUPS, TOKENS, HEADS * DH)
    query_part = jnp.clip(jax.random.normal(jax.random.fold_in(key, 101), shape_all, jnp.float32), -5.0, 5.0)
    key_part = jnp.clip(jax.random.normal(jax.random.fold_in(key, 102), shape_all, jnp.float32), -5.0, 5.0)
    return (query_part, key_part)


def draw_query(key, part):
    query_part, key_part = paired_draw(key)
    return query_part.astype(jnp.bfloat16)


def draw_key_in(key, part):
    query_part, key_part = paired_draw(key)
    return key_part.astype(jnp.bfloat16)


def scaled_rows(key, salt, row_count, col_count):
    normal_part = jnp.clip(jax.random.normal(jax.random.fold_in(key, salt), (HEADS, row_count, col_count), jnp.float32), -5.0, 5.0)
    position = jnp.arange(row_count, dtype=jnp.float32) / max(row_count - 1, 1)
    scales = jnp.exp(jnp.log(3.0) * position)
    return (normal_part * scales[None, :, None]).astype(jnp.bfloat16)


def draw_w_in(key, part):
    return scaled_rows(key, 201, DH, HID)


def draw_w_gate(key, part):
    return scaled_rows(key, 202, DH, HID)


def draw_w_out(key, part):
    return scaled_rows(key, 203, HID, DH)


def with_spikes(values, key, source, target, blocks, factor):
    def block_of(axis_at):
        return (jnp.arange(values.shape[axis_at]) // (values.shape[axis_at] // blocks)).reshape((-1,) + (1,) * (values.ndim - 1 - axis_at))

    near = jax.random.permutation(key, blocks)[block_of(target)]
    other_side = (block_of(target) + blocks // 2) % blocks
    return jnp.where((block_of(source) == near) | (block_of(source) == other_side), factor * values, values)


def shard_levels(own_key, dims, pieces, smallest, high):
    level = 1.0
    for dim, shards_of in pieces:
        heights = jax.random.uniform(jax.random.fold_in(jax.random.fold_in(own_key, 6), dim), (shards_of,), jnp.float32, smallest / len(pieces), high / len(pieces))
        level = level * jnp.repeat(jnp.exp(heights), dims[dim] // shards_of).reshape((-1,) + (1,) * (len(dims) - 1 - dim))
    return level


def centred(key, extent, scale, most, split=(), kind=jnp.bfloat16):
    loudness = shard_levels(key, extent, split, -0.22, 0.18) if split else 1.0
    entries = jax.random.normal(key, extent, jnp.float32) * scale * loudness
    return jnp.minimum(jnp.maximum(entries, -most), most).astype(kind)


def bell_draw_with(rng, extent, deviation, limit, split, heavy, held_as=jnp.bfloat16):
    array = deviation * jax.random.normal(rng, extent, jnp.float32)
    if split:
        array = array * shard_levels(rng, extent, split, -0.22, 0.18)
    return jnp.clip(with_spikes(array, jax.random.fold_in(rng, 3), *heavy), -limit, limit).astype(held_as)


def setup_inputs(seed: int = 0) -> dict:
    splits = jax.random.split(jax.random.key(seed), 10)
    return {
        "query": draw_query(jax.random.fold_in(splits[9], 71), 0),
        "key_in": draw_key_in(jax.random.fold_in(splits[9], 71), 0),
        "value": centred(splits[2], (GROUPS, TOKENS, HEADS * DH), 1.0, 6.0, ((1, 32), (2, 8))),
        "rates": jnp.clip(jnp.exp(math.log(0.3) - 2.3025852 * jax.random.uniform(splits[3], (GROUPS, HEADS, TOKENS), jnp.float32) ** shard_levels(splits[3], (GROUPS, HEADS, TOKENS), ((1, 8), (2, 32)), -0.2, 0.2)), 0.03, 0.3),
        "w_in": draw_w_in(jax.random.fold_in(splits[9], 71), 0),
        "w_gate": draw_w_gate(jax.random.fold_in(splits[9], 71), 0),
        "w_out": draw_w_out(jax.random.fold_in(splits[9], 71), 0),
        "norm_gain": jnp.clip(1.0 + 0.18 * jax.random.normal(splits[7], (HEADS, DH), jnp.float32), 0.1, 1.9),
        "proj_weight": bell_draw_with(splits[8], (HEADS * DH, MODEL), (HEADS * DH) ** -0.5, 0.125, ((0, 8),), (0, 1, 8, 2.0)),
    }


def silu_pair(inputs):
    sigmoid = jax.nn.sigmoid(inputs)
    return (inputs * sigmoid, sigmoid * (1.0 + inputs * (1.0 - sigmoid)))

def window_attention(query_rows, key_rows, value_rows):
    half_window = WINDOW // 2
    block = min(512, TOKENS)
    keys_pad = jnp.pad(key_rows, ((half_window, half_window), (0, 0)))
    values_pad = jnp.pad(value_rows, ((half_window, half_window), (0, 0)))
    row_ids = jnp.arange(block, dtype=jnp.int32)[:, None]
    col_ids = jnp.arange(block + WINDOW, dtype=jnp.int32)[None, :]

    def one_block(block_idx):
        offset = (block_idx * block).astype(jnp.int32)
        query_blk = lax.dynamic_slice_in_dim(query_rows, offset, block, 0)
        key_blk = lax.dynamic_slice_in_dim(keys_pad, offset, block + WINDOW, 0)
        value_blk = lax.dynamic_slice_in_dim(values_pad, offset, block + WINDOW, 0)
        scores = jnp.dot(query_blk, key_blk.T, preferred_element_type=jnp.float32) * DH ** (-0.5)
        key_glob = offset + col_ids - half_window
        valid = (col_ids - row_ids >= 0) & (col_ids - row_ids < WINDOW) & (key_glob >= 0) & (key_glob < TOKENS)
        scores = jnp.where(valid, scores, -1e+30)
        largest = lax.optimization_barrier(jnp.max(scores, axis=1, keepdims=True))
        expo = jnp.exp(scores - largest)
        probs = expo / lax.optimization_barrier(jnp.sum(expo, axis=1, keepdims=True))
        return jnp.dot(probs.astype(jnp.bfloat16), value_blk, preferred_element_type=jnp.float32)
    outputs = lax.map(one_block, jnp.arange(TOKENS // block, dtype=jnp.int32))
    return outputs.reshape(TOKENS, DH)

def head_step(inputs):
    query_rows, key_rows, value_rows, rate_row, weights_in, weights_gate, weights_out, gain_row = inputs
    scale_in = DH ** (-0.5)
    scale_out = HID ** (-0.5)
    bf_in = weights_in.astype(jnp.bfloat16)
    bf_gate = weights_gate.astype(jnp.bfloat16)
    bf_out = weights_out.astype(jnp.bfloat16)
    first_pre = jnp.dot(query_rows, bf_in, preferred_element_type=jnp.float32) * scale_in
    gate_pre = jnp.dot(query_rows, bf_gate, preferred_element_type=jnp.float32) * scale_in
    first_act, unused = silu_pair(first_pre)
    hidden_q = (first_act * gate_pre).astype(jnp.bfloat16)
    ttt_out = jnp.dot(hidden_q, bf_out, preferred_element_type=jnp.float32) * scale_out
    normed = ttt_out * lax.rsqrt(lax.optimization_barrier(jnp.mean(ttt_out * ttt_out, axis=1, keepdims=True)) + 1e-06) * gain_row[None, :]
    window = window_attention(query_rows, key_rows, value_rows)
    head_out = (normed + window).astype(jnp.bfloat16)
    key_first = jnp.dot(key_rows, bf_in, preferred_element_type=jnp.float32) * scale_in
    key_gate = jnp.dot(key_rows, bf_gate, preferred_element_type=jnp.float32) * scale_in
    key_act, key_slope = silu_pair(key_first)
    hidden_k = (key_act * key_gate).astype(jnp.bfloat16)
    scaled = (rate_row[:, None] * value_rows.astype(jnp.float32)).astype(jnp.bfloat16)
    grad_out = -scale_out * jnp.dot(hidden_k.T, scaled, preferred_element_type=jnp.float32)
    back = -scale_out * jnp.dot(scaled, bf_out.T, preferred_element_type=jnp.float32)
    delta_in = (back * key_gate * key_slope).astype(jnp.bfloat16)
    delta_gate = (back * key_act).astype(jnp.bfloat16)
    grad_in = scale_in * jnp.dot(key_rows.T, delta_in, preferred_element_type=jnp.float32)
    grad_gate = scale_in * jnp.dot(key_rows.T, delta_gate, preferred_element_type=jnp.float32)
    return (head_out, grad_in, grad_gate, grad_out)

def renormalize(updated, before):
    kept = jnp.sqrt(lax.optimization_barrier(jnp.sum(before * before, axis=-2, keepdims=True)))
    return updated * (kept / jnp.sqrt(lax.optimization_barrier(jnp.sum(updated * updated, axis=-2, keepdims=True)) + 1e-06))

def add_head(total, inputs):
    head_rows, proj_rows = inputs
    partial_value = jnp.dot(head_rows, proj_rows, preferred_element_type=jnp.float32)
    rounded = lax.optimization_barrier(partial_value.astype(jnp.bfloat16)).astype(jnp.float32)
    return (total + rounded, None)

def reference(query, key_in, value, rates, w_in, w_gate, w_out, norm_gain, proj_weight):
    state_in = w_in.astype(jnp.float32)
    state_gate = w_gate.astype(jnp.float32)
    state_out = w_out.astype(jnp.float32)
    proj_heads = proj_weight.reshape(HEADS, DH, MODEL)
    mixed_list = []
    for group_idx in range(GROUPS):
        query_heads = query[group_idx].reshape(TOKENS, HEADS, DH).transpose(1, 0, 2)
        key_heads = key_in[group_idx].reshape(TOKENS, HEADS, DH).transpose(1, 0, 2)
        value_heads = value[group_idx].reshape(TOKENS, HEADS, DH).transpose(1, 0, 2)
        head_outs, grad_in, grad_gate, grad_out = lax.map(head_step, (query_heads, key_heads, value_heads, rates[group_idx], state_in, state_gate, state_out, norm_gain))
        total, unused = lax.scan(add_head, jnp.zeros((TOKENS, MODEL), jnp.float32), (head_outs, proj_heads))
        mixed_list.append(total.astype(jnp.bfloat16))
        state_in = renormalize(state_in - grad_in, state_in)
        state_gate = renormalize(state_gate - grad_gate, state_gate)
        state_out = renormalize(state_out - grad_out, state_out)
    mixed = jnp.stack(mixed_list, axis=0)
    return (mixed, state_in.astype(jnp.bfloat16), state_gate.astype(jnp.bfloat16), state_out.astype(jnp.bfloat16))
```

```python
import functools

import jax
import jax.numpy as jnp
from jax import lax
from jax.experimental import pallas as pl
from jax.experimental.pallas import tpu as pltpu
from jax.sharding import PartitionSpec as P

DH = 512
HID = 512
HALF = HID // 2
GROUPS = 2
WINDOW = 1024
SIDE = WINDOW // 2
A = DH**-0.5
B = HID**-0.5
BF = jnp.bfloat16
F32 = jnp.float32


def dot(x, y, dims=((1,), (0,))):
    return lax.dot_general(x, y, (dims, ((), ())), preferred_element_type=F32)


def kernel(
    chips,
    ys,
    q_hbm,
    k_hbm,
    v_hbm,
    rates_ref,
    w1_ref,
    w3_ref,
    w2_ref,
    gain_ref,
    proj_hbm,
    mixed_ref,
    out1_ref,
    out3_ref,
    out2_ref,
    qs,
    kx,
    vx,
    rx,
    s13,
    s2,
    b13,
    b2,
    acc13,
    acc2,
    win,
    part,
    landed,
    total,
    gathered,
    heads,
    pw,
    xs,
    xr,
    xa,
    loc_sem,
    sib_s,
    sib_r,
    far_s,
    far_r,
    rs_s,
    rs_r,
    ag_s,
    ag_r,
    ex_s,
    ex_r,
    w_s,
    w_r,
    ws_s,
    ws_r,
    y_s,
    y_r,
    x_s,
    x_r,
):
    tok = kx.shape[1] - 2 * SIDE
    ctx = lax.axis_index("ctx")
    head = lax.axis_index("head")
    n_ctx = 2 * chips
    core = lax.rem(ctx, 2)
    chip = lax.div(ctx, 2)
    y = lax.div(head, 2)
    x_lo = lax.rem(head, 2)
    sib = (ctx + 1 - 2 * core, head)
    far = (lax.rem(ctx + 2 * core - 1 + n_ctx, n_ctx), head)
    pair = (ctx, head + 1 - 2 * x_lo)

    def chip_peer(d):
        return (lax.rem(chip + d, chips) * 2 + core, head)

    def y_peer(d):
        return (ctx, lax.rem(y + d, ys) * 2 + x_lo)

    peers = [sib, far, pair] + [chip_peer(d) for d in range(1, chips)] + [y_peer(d) for d in range(1, ys)]

    def local_copy(src, dst, n):
        c = pltpu.make_async_copy(src, dst, loc_sem.at[n])
        c.start()
        return c

    waiting = []

    def remote(src, dst, send, recv, peer):
        c = pltpu.make_async_remote_copy(
            src_ref=src, dst_ref=dst, send_sem=send, recv_sem=recv, device_id=peer, device_id_type=pl.DeviceIdType.MESH
        )
        c.start()
        waiting.append(c)
        return c

    own = pl.ds(SIDE, tok)
    my_half = pl.ds(pl.multiple_of(core * HALF, HALF), HALF)

    loads_k = [local_copy(k_hbm.at[g], kx.at[g, own], g) for g in range(GROUPS)]
    loads_v = [local_copy(v_hbm.at[g], vx.at[g, own], GROUPS + g) for g in range(GROUPS)]
    load_q = local_copy(q_hbm, qs, 2 * GROUPS)
    load_p = local_copy(proj_hbm.at[:, pl.ds(pl.multiple_of(y * 1280, 1280), 1280)], pw.at[0], 2 * GROUPS + 1)

    barrier = pltpu.get_barrier_semaphore()
    for peer in peers:
        pl.semaphore_signal(barrier, inc=1, device_id=peer, device_id_type=pl.DeviceIdType.MESH)
    pl.semaphore_wait(barrier, len(peers))

    to_sib = pl.ds(pl.multiple_of(core * WINDOW, SIDE), SIDE)
    to_far = pl.ds(pl.multiple_of((1 - core) * WINDOW, SIDE), SIDE)
    from_sib = pl.ds(pl.multiple_of((1 - core) * WINDOW, SIDE), SIDE)

    rate_copy = remote(rates_ref, rx, sib_s.at[2 * GROUPS], sib_r.at[2 * GROUPS], sib)
    sib_copies, far_copies = [], []
    for g in range(GROUPS):
        sib_copies.append(
            (
                remote(k_hbm.at[g], kx.at[g, to_sib], sib_s.at[2 * g], sib_r.at[2 * g], sib),
                remote(v_hbm.at[g], vx.at[g, to_sib], sib_s.at[2 * g + 1], sib_r.at[2 * g + 1], sib),
            )
        )
        far_copies.append(
            (
                remote(k_hbm.at[g], kx.at[g, to_far], far_s.at[2 * g], far_r.at[2 * g], far),
                remote(v_hbm.at[g], vx.at[g, to_far], far_s.at[2 * g + 1], far_r.at[2 * g + 1], far),
            )
        )
    w_copies = []
    for d in range(1, ys):
        cols = pl.ds(pl.multiple_of(lax.rem(y + d, ys) * 1280, 1280), 1280)
        w_copies.append(remote(proj_hbm.at[my_half, cols], pw.at[d, my_half], w_s.at[d], w_r.at[d], y_peer(d)))

    for c in range(2):
        cols = slice(c * HALF, (c + 1) * HALF)
        for j, w in enumerate((w1_ref, w3_ref)):
            into = slice(j * HALF, (j + 1) * HALF)
            b13[c, :, into] = w[:, cols]
            s13[c, :, into] = w[:, cols].astype(F32)
    b2[...] = w2_ref[...]
    s2[...] = w2_ref[...].astype(F32)

    def key_part(g, rows, rate_row, first):
        k = kx[g, rows]
        v = vx[g, rows]
        f = dot(k, b13[core]) * A
        f1, f3 = f[:, :HALF], f[:, HALF:]
        sig = jax.nn.sigmoid(f1)
        act = f1 * sig
        slope = sig * (1.0 + f1 * (1.0 - sig))
        hk = (act * f3).astype(BF)
        rate = jnp.transpose(jnp.broadcast_to(rate_row, (128, tok)))[:, :1]
        scaled = (v.astype(F32) * rate).astype(BF)
        back = dot(scaled, b2[my_half], ((1,), (1,))) * -B
        d13 = jnp.concatenate([(back * f3 * slope).astype(BF), (back * act).astype(BF)], axis=1)
        g2 = dot(hk, scaled, ((0,), (0,))) * -B
        g13 = dot(k, d13, ((0,), (0,))) * A
        if first:
            acc13[...] = g13
            acc2[...] = g2
        else:
            rows13, rows2 = DH // chips, HALF // chips
            part[g, :, :rows13] = (acc13[...] + g13).reshape(chips, rows13, 2 * HALF).astype(BF)
            part[g, :, rows13:] = (acc2[...] + g2).reshape(chips, rows2, DH).astype(BF)

    def gradients(g):
        if g == 0:
            loads_k[0].wait()
            loads_v[0].wait()
        key_part(g, own, rates_ref[g : g + 1], True)
        if g == 0:
            rate_copy.wait_recv()
            for c in sib_copies[0]:
                c.wait_recv()
        key_part(g, from_sib, rx[g : g + 1], False)
        return [
            remote(part.at[g, lax.rem(chip + d, chips)], landed.at[g, d], rs_s.at[g, d], rs_r.at[g, d], chip_peer(d))
            for d in range(1, chips)
        ]

    def reduce_own(g, copies):
        for c in copies:
            c.wait_recv()
        s = part[g, chip].astype(F32)
        for d in range(1, chips):
            s += landed[g, d].astype(F32)
        total[g] = s.astype(BF)
        gathered[g, core, chip] = total[g]
        return [
            remote(total.at[g], gathered.at[g, core, chip], ag_s.at[g, d], ag_r.at[g, d], chip_peer(d))
            for d in range(1, chips)
        ]

    def exchange(g, copies):
        for c in copies:
            c.wait_recv()
        return remote(gathered.at[g, core], gathered.at[g, core], ex_s.at[g], ex_r.at[g], sib)

    def rescaled(before, grad):
        changed = before - grad
        kept = jnp.sqrt(jnp.sum(before * before, axis=0, keepdims=True))
        return changed * (kept / jnp.sqrt(jnp.sum(changed * changed, axis=0, keepdims=True) + 1e-6))

    def update(g, copy):
        copy.wait_recv()
        rows13 = DH // chips
        for c in range(2):
            grad = gathered[g, c, :, :rows13].astype(F32).reshape(DH, 2 * HALF)
            new = rescaled(s13[c], grad)
            s13[c] = new
            b13[c] = new.astype(BF)
        grad = gathered[g, :, :, rows13:].astype(F32).reshape(HID, DH)
        new = rescaled(s2[...], grad)
        s2[...] = new
        b2[...] = new.astype(BF)

    block = 256
    width = block + WINDOW

    def attend(g):
        if g > 0:
            loads_k[g].wait()
            loads_v[g].wait()
        for c in far_copies[g]:
            c.wait_recv()
        if g > 0:
            for c in sib_copies[g]:
                c.wait_recv()

        @pl.loop(0, tok // block)
        def _(i):
            start = pl.multiple_of(i * block, block)
            q = qs[g, pl.ds(start, block)]
            s = dot(q, kx[g, pl.ds(start, width)], ((1,), (1,))) * A
            row = lax.broadcasted_iota(jnp.int32, (block, width), 0)
            col = lax.broadcasted_iota(jnp.int32, (block, width), 1)
            at = ctx * tok + start - SIDE + col
            seen = (col - row >= 0) & (col - row < WINDOW) & (at >= 0) & (at < n_ctx * tok)
            s = jnp.where(seen, s, -1e30)
            e = jnp.exp(s - jnp.max(s, axis=1, keepdims=True))
            o = dot(e.astype(BF), vx[g, pl.ds(start, width)])
            win[g, pl.ds(start, block)] = o / jnp.sum(e, axis=1, keepdims=True)

    def hidden(g, c):
        f = dot(qs[g], b13[c]) * A
        f1 = f[:, :HALF]
        return (f1 * jax.nn.sigmoid(f1) * f[:, HALF:]).astype(BF)

    def head_out(g):
        h = jnp.concatenate([hidden(g, 0), hidden(g, 1)], axis=1)
        t = dot(h, b2[...]) * B
        normed = t * lax.rsqrt(jnp.mean(t * t, axis=1, keepdims=True) + 1e-6) * gain_ref[...]
        heads[g, 0] = (normed + win[g]).astype(BF)
        return [remote(heads.at[g, 0], heads.at[g, d], y_s.at[g, d], y_r.at[g, d], y_peer(d)) for d in range(1, ys)]

    def project(g, copies):
        for c in copies:
            c.wait_recv()
        wide = 640
        for mine in (False, True):
            def cols_of(which):
                return slice(which * wide, (which + 1) * wide)

            for which in range(2):
                @pl.when((x_lo == which) if mine else (x_lo != which))
                def _():
                    t = dot(heads[g, 0], pw[0, :, cols_of(which)])
                    for d in range(1, ys):
                        t += dot(heads[g, d], pw[d, :, cols_of(which)])
                    if mine:
                        xa[g] = t
                    else:
                        xs[g] = t.astype(BF)

            if not mine:
                sent = remote(xs.at[g], xr.at[g], x_s.at[g], x_r.at[g], pair)
        return sent

    reducing = gradients(0)
    load_q.wait()
    attend(0)
    y_copies0 = head_out(0)
    summed = reduce_own(0, reducing)
    attend(1)
    ex = exchange(0, summed)
    update(0, ex)
    reducing = gradients(1)
    y_copies1 = head_out(1)
    w_forward = []
    for d in range(1, ys):
        w_copies[d - 1].wait_recv()
        w_forward.append(remote(pw.at[d, my_half], pw.at[d, my_half], ws_s.at[d], ws_r.at[d], sib))
    summed = reduce_own(1, reducing)
    load_p.wait()
    for c in w_forward:
        c.wait_recv()
    sent0 = project(0, y_copies0)
    ex = exchange(1, summed)
    sent1 = project(1, y_copies1)
    update(1, ex)
    for c in range(2):
        cols = slice(c * HALF, (c + 1) * HALF)
        out1_ref[:, cols] = b13[c, :, :HALF]
        out3_ref[:, cols] = b13[c, :, HALF:]
    out2_ref[...] = b2[...]
    for g, sent in ((0, sent0), (1, sent1)):
        sent.wait_recv()
        mixed_ref[g] = (xa[g] + xr[g].astype(F32)).astype(BF)
    for c in waiting:
        c.wait_send()


def local(query, key_in, value, rates, w_in, w_gate, w_out, norm_gain, proj_weight):
    tok = query.shape[1]
    chips = lax.axis_size("ctx") // 2
    ys = lax.axis_size("head") // 2
    piece = DH // chips + HALF // chips
    vmem = pl.BlockSpec(memory_space=pltpu.VMEM)
    hbm = pl.BlockSpec(memory_space=pl.ANY)
    dma = pltpu.SemaphoreType.DMA
    ext = tok + WINDOW
    mixed, new1, new3, new2 = pl.pallas_call(
        functools.partial(kernel, chips, ys),
        out_shape=(
            jax.ShapeDtypeStruct((GROUPS, tok, 640), BF),
            jax.ShapeDtypeStruct((DH, HID), BF),
            jax.ShapeDtypeStruct((DH, HID), BF),
            jax.ShapeDtypeStruct((HID, DH), BF),
        ),
        in_specs=[hbm, hbm, hbm, vmem, vmem, vmem, vmem, vmem, hbm],
        out_specs=(vmem, vmem, vmem, vmem),
        scratch_shapes=[
            pltpu.VMEM((GROUPS, tok, DH), BF),
            pltpu.VMEM((GROUPS, ext, DH), BF),
            pltpu.VMEM((GROUPS, ext, DH), BF),
            pltpu.VMEM((GROUPS, tok), F32),
            pltpu.VMEM((2, DH, 2 * HALF), F32),
            pltpu.VMEM((HID, DH), F32),
            pltpu.VMEM((2, DH, 2 * HALF), BF),
            pltpu.VMEM((HID, DH), BF),
            pltpu.VMEM((DH, 2 * HALF), F32),
            pltpu.VMEM((HALF, DH), F32),
            pltpu.VMEM((GROUPS, tok, DH), F32),
            pltpu.VMEM((GROUPS, chips, piece, DH), BF),
            pltpu.VMEM((GROUPS, chips, piece, DH), BF),
            pltpu.VMEM((GROUPS, piece, DH), BF),
            pltpu.VMEM((GROUPS, 2, chips, piece, DH), BF),
            pltpu.VMEM((GROUPS, ys, tok, DH), BF),
            pltpu.VMEM((ys, DH, 1280), BF),
            pltpu.VMEM((GROUPS, tok, 640), BF),
            pltpu.VMEM((GROUPS, tok, 640), BF),
            pltpu.VMEM((GROUPS, tok, 640), F32),
            dma((2 * GROUPS + 2,)),
            dma((2 * GROUPS + 1,)),
            dma((2 * GROUPS + 1,)),
            dma((2 * GROUPS,)),
            dma((2 * GROUPS,)),
            dma((GROUPS, chips)),
            dma((GROUPS, chips)),
            dma((GROUPS, chips)),
            dma((GROUPS, chips)),
            dma((GROUPS,)),
            dma((GROUPS,)),
            dma((ys,)),
            dma((ys,)),
            dma((ys,)),
            dma((ys,)),
            dma((GROUPS, ys)),
            dma((GROUPS, ys)),
            dma((GROUPS,)),
            dma((GROUPS,)),
        ],
        compiler_params=pltpu.CompilerParams(
            collective_id=0, has_side_effects=True, vmem_limit_bytes=60 * 1024 * 1024
        ),
    )(
        query,
        key_in,
        value,
        rates[:, 0],
        w_in[0],
        w_gate[0],
        w_out[0],
        norm_gain,
        proj_weight,
    )
    return mixed, new1[None], new3[None], new2[None]


def solution(mesh):
    return jax.shard_map(
        local,
        mesh=mesh,
        in_specs=(
            P(None, "ctx", "head"),
            P(None, "ctx", "head"),
            P(None, "ctx", "head"),
            P(None, "head", "ctx"),
            P("head", None, None),
            P("head", None, None),
            P("head", None, None),
            P("head", None),
            P("head", None),
        ),
        out_specs=(
            P(None, "ctx", "head"),
            P("head", None, None),
            P("head", None, None),
            P("head", None, None),
        ),
        check_vma=False,
    )
```

```python
import functools

import jax
import jax.numpy as jnp
from jax import lax
from jax.experimental import pallas as pl
from jax.experimental.pallas import tpu as pltpu
from jax.sharding import PartitionSpec as P

DH = 512
HID = 512
HALF = HID // 2
GROUPS = 2
WINDOW = 1024
SIDE = WINDOW // 2
A = DH**-0.5
B = HID**-0.5
CHUNKS = 2
FAR_PARTS = 4
BF = jnp.bfloat16
F32 = jnp.float32


def dot(x, y, dims=((1,), (0,))):
    return lax.dot_general(x, y, (dims, ((), ())), preferred_element_type=F32)


def kernel(
    zs,
    ys,
    q_hbm,
    k_hbm,
    v_hbm,
    rates_ref,
    w1_ref,
    w3_ref,
    w2_ref,
    gain_ref,
    proj_hbm,
    mixed_ref,
    out1_ref,
    out3_ref,
    out2_ref,
    qs,
    kx,
    vx,
    rx,
    s13,
    s2,
    b13,
    b2,
    kept13,
    kept2,
    acc13,
    acc2,
    hq,
    normed,
    part,
    landed,
    mine,
    theirs,
    gathered,
    heads,
    pw,
    xs,
    xr,
    xa,
    loc_sem,
    sib_s,
    sib_r,
    far_s,
    far_r,
    rs_s,
    rs_r,
    hi_s,
    hi_r,
    ag_s,
    ag_r,
    ex_s,
    ex_r,
    w_s,
    w_r,
    ws_s,
    ws_r,
    y_s,
    y_r,
    x_s,
    x_r,
):
    tok = kx.shape[1] - 2 * SIDE
    wide = xs.shape[-1]
    block = tok // CHUNKS
    rows13, rows2 = DH // zs, HALF // zs
    piece = rows13 + rows2
    ctx = lax.axis_index("ctx")
    head = lax.axis_index("head")
    n_ctx = 4 * zs
    core = lax.rem(ctx, 2)
    x_hi = lax.rem(lax.div(ctx, 2), 2)
    z = lax.div(ctx, 4)
    y = lax.div(head, 2)
    x_lo = lax.rem(head, 2)
    sib = (ctx + 1 - 2 * core, head)
    far = (lax.rem(ctx + 2 * core - 1 + n_ctx, n_ctx), head)
    pair = (ctx, head + 1 - 2 * x_lo)
    across = (ctx + 2 - 4 * x_hi, head)

    def z_at(d):
        return lax.rem(z + d + zs, zs)

    along = [(z_at(d) * 4 + x_hi * 2 + core, head) for d in (1, -1)]

    def y_peer(d):
        return (ctx, lax.rem(y + d, ys) * 2 + x_lo)

    peers = [sib, far, pair, across] + along + [y_peer(d) for d in range(1, ys)]

    def local_copy(src, dst, n):
        c = pltpu.make_async_copy(src, dst, loc_sem.at[n])
        c.start()
        return c

    waiting = []

    def remote(src, dst, send, recv, peer):
        c = pltpu.make_async_remote_copy(
            src_ref=src, dst_ref=dst, send_sem=send, recv_sem=recv, device_id=peer, device_id_type=pl.DeviceIdType.MESH
        )
        c.start()
        waiting.append(c)
        return c

    own = pl.ds(SIDE, tok)
    my_half = pl.ds(pl.multiple_of(core * HALF, HALF), HALF)

    loads_k = [local_copy(k_hbm.at[g], kx.at[g, own], g) for g in range(GROUPS)]
    loads_v = [local_copy(v_hbm.at[g], vx.at[g, own], GROUPS + g) for g in range(GROUPS)]
    load_q = local_copy(q_hbm, qs, 2 * GROUPS)
    load_p = local_copy(
        proj_hbm.at[:, pl.ds(pl.multiple_of(y * 2 * wide, 2 * wide), 2 * wide)], pw.at[0], 2 * GROUPS + 1
    )

    barrier = pltpu.get_barrier_semaphore()
    for peer in peers:
        pl.semaphore_signal(barrier, inc=1, device_id=peer, device_id_type=pl.DeviceIdType.MESH)
    pl.semaphore_wait(barrier, len(peers))

    to_sib = pl.ds(pl.multiple_of(core * WINDOW, SIDE), SIDE)
    from_sib = pl.ds(pl.multiple_of((1 - core) * WINDOW, SIDE), SIDE)

    def send_rows(g):
        return [
            remote(k_hbm.at[g], kx.at[g, to_sib], sib_s.at[2 * g], sib_r.at[2 * g], sib),
            remote(v_hbm.at[g], vx.at[g, to_sib], sib_s.at[2 * g + 1], sib_r.at[2 * g + 1], sib),
        ]

    far_copies = [[], []]
    far_rows = tok // FAR_PARTS

    def send_far(g, parts):
        for n in parts:
            rows = pl.ds(pl.multiple_of((1 - core) * WINDOW + n * far_rows, far_rows), far_rows)
            for j, (src, dst) in enumerate(((k_hbm, kx), (v_hbm, vx))):
                far_copies[g].append(
                    remote(
                        src.at[g, n * far_rows : (n + 1) * far_rows],
                        dst.at[g, rows],
                        far_s.at[g, j, n],
                        far_r.at[g, j, n],
                        far,
                    )
                )

    rate_copy = remote(rates_ref, rx, sib_s.at[2 * GROUPS], sib_r.at[2 * GROUPS], sib)
    sib_copies = [send_rows(0)]
    send_far(0, (0, 1))
    sib_copies.append(send_rows(1))
    w_copies = []

    def send_weights(d):
        cols = pl.ds(pl.multiple_of(lax.rem(y + d, ys) * 2 * wide, 2 * wide), 2 * wide)
        w_copies.append(remote(proj_hbm.at[my_half, cols], pw.at[d, my_half], w_s.at[d], w_r.at[d], y_peer(d)))

    def column_norm(x):
        return jnp.sqrt(jnp.sum(x * x, axis=0, keepdims=True))

    for c in range(2):
        cols = slice(c * HALF, (c + 1) * HALF)
        for j, w in enumerate((w1_ref, w3_ref)):
            into = slice(j * HALF, (j + 1) * HALF)
            b13[c, :, into] = w[:, cols]
            s13[c, :, into] = w[:, cols].astype(F32)
    b2[...] = w2_ref[...]
    s2[...] = w2_ref[...].astype(F32)

    def norms():
        for c in range(2):
            kept13[c] = column_norm(s13[c])
        kept2[...] = column_norm(s2[...])

    def key_part(g, rows, rate_row, first):
        k = kx[g, rows]
        v = vx[g, rows]
        f = dot(k, b13[core]) * A
        f1, f3 = f[:, :HALF], f[:, HALF:]
        sig = jax.nn.sigmoid(f1)
        act = f1 * sig
        slope = sig * (1.0 + f1 * (1.0 - sig))
        hk = (act * f3).astype(BF)
        rate = jnp.transpose(jnp.broadcast_to(rate_row, (128, tok)))[:, :1]
        scaled = (v.astype(F32) * rate).astype(BF)
        back = dot(scaled, b2[my_half], ((1,), (1,))) * -B
        d13 = jnp.concatenate([(back * f3 * slope).astype(BF), (back * act).astype(BF)], axis=1)
        g2 = dot(hk, scaled, ((0,), (0,))) * -B
        g13 = dot(k, d13, ((0,), (0,))) * A
        if first:
            acc13[...] = g13
            acc2[...] = g2
        else:
            part[g, :, :rows13] = (acc13[...] + g13).reshape(zs, rows13, 2 * HALF).astype(BF)
            part[g, :, rows13:] = (acc2[...] + g2).reshape(zs, rows2, DH).astype(BF)

    def gradients(g):
        if g == 0:
            loads_k[0].wait()
            loads_v[0].wait()
        else:
            arrived(1)
        key_part(g, own, rates_ref[g : g + 1], True)
        if g == 0:
            rate_copy.wait_recv()
            for c in sib_copies[0]:
                c.wait_recv()
        key_part(g, from_sib, rx[g : g + 1], False)

    sub = piece // 2
    steps = zs // 2
    flows = ((0, 0), (1, 1), (0, 1), (1, 0))

    def rows_of(h):
        return pl.ds(h * sub, sub)

    def sum_gradients(g):
        last = {}
        for s in range(1, steps + 1):
            now = {}
            for way, h in flows:
                if s == 1 and way != h:
                    continue
                target = z_at((steps + 1 - s) * (1 - 2 * way))
                if (way, h) in last:
                    last[way, h].wait_recv()
                    got = landed[g, way, s - 2, h].astype(F32) + part[g, target, rows_of(h)].astype(F32)
                    landed[g, way, s - 2, h] = got.astype(BF)
                    src = landed.at[g, way, s - 2, h]
                else:
                    src = part.at[g, target, rows_of(h)]
                now[way, h] = remote(
                    src, landed.at[g, way, s - 1, h], rs_s.at[g, way, s - 1, h], rs_r.at[g, way, s - 1, h], along[way]
                )
            last = now
            yield
        swaps = []
        for h in range(2):
            for way in range(2):
                last[way, h].wait_recv()
            got = landed[g, 0, steps - 1, h].astype(F32) + landed[g, 1, steps - 1, h].astype(F32)
            mine[g, h] = (got + part[g, z, rows_of(h)].astype(F32)).astype(BF)
            swaps.append(remote(mine.at[g, h], theirs.at[g, h], hi_s.at[g, h], hi_r.at[g, h], across))
        yield
        exchanged = []

        def to_sibling(origin, h, n):
            at = gathered.at[g, core, origin, rows_of(h)]
            exchanged.append(remote(at, at, ex_s.at[g, n, h], ex_r.at[g, n, h], sib))

        last = {}
        for h in range(2):
            swaps[h].wait_recv()
            gathered[g, core, z, rows_of(h)] = (mine[g, h].astype(F32) + theirs[g, h].astype(F32)).astype(BF)
            for way in range(2):
                at = gathered.at[g, core, z, rows_of(h)]
                last[way, h] = remote(at, at, ag_s.at[g, way, 0, h], ag_r.at[g, way, 0, h], along[way])
            to_sibling(z, h, 0)
        yield
        for s in range(2, steps + 1):
            now = {}
            for way, h in flows:
                last[way, h].wait_recv()
                origin = z_at((s - 1) * (2 * way - 1))
                if s < steps or way == h:
                    at = gathered.at[g, core, origin, rows_of(h)]
                    now[way, h] = remote(
                        at, at, ag_s.at[g, way, s - 1, h], ag_r.at[g, way, s - 1, h], along[way]
                    )
                to_sibling(origin, h, 2 * (s - 1) - 1 + way)
            last = now
            yield
        for way in range(2):
            last[way, way].wait_recv()
            to_sibling(z_at(steps), way, zs - 1)
        for c in exchanged:
            c.wait_recv()

    def update(g):
        def rescaled(before, grad, kept):
            changed = before - grad
            return changed * (kept / jnp.sqrt(jnp.sum(changed * changed, axis=0, keepdims=True) + 1e-6))

        final = g == GROUPS - 1
        for c in range(2):
            grad = gathered[g, c, :, :rows13].astype(F32).reshape(DH, 2 * HALF)
            new = rescaled(s13[c], grad, kept13[c])
            if final:
                out1_ref[:, c * HALF : (c + 1) * HALF] = new[:, :HALF].astype(BF)
                out3_ref[:, c * HALF : (c + 1) * HALF] = new[:, HALF:].astype(BF)
            else:
                s13[c] = new
                b13[c] = new.astype(BF)
        grad = gathered[g, :, :, rows13:].astype(F32).reshape(HID, DH)
        new = rescaled(s2[...], grad, kept2[...])
        if final:
            out2_ref[...] = new.astype(BF)
        else:
            s2[...] = new
            b2[...] = new.astype(BF)

    done = set()

    def arrived(g):
        if g not in done:
            done.add(g)
            loads_k[g].wait()
            loads_v[g].wait()
            for c in sib_copies[g]:
                c.wait_recv()

    def hidden(g, c):
        f = dot(qs[g], b13[c]) * A
        f1 = f[:, :HALF]
        hq[:, c * HALF : (c + 1) * HALF] = (f1 * jax.nn.sigmoid(f1) * f[:, HALF:]).astype(BF)

    def fast_out():
        t = dot(hq[...], b2[...]) * B
        normed[...] = t * lax.rsqrt(jnp.mean(t * t, axis=1, keepdims=True) + 1e-6) * gain_ref[...]

    width = block + WINDOW
    y_copies = {}

    def attend(g, i):
        if i == 0:
            for c in far_copies[g]:
                c.wait_recv()
        start = i * block
        rows = slice(start, start + block)
        s = dot(qs[g, rows], kx[g, start : start + width], ((1,), (1,))) * A
        row = lax.broadcasted_iota(jnp.int32, (block, width), 0)
        col = lax.broadcasted_iota(jnp.int32, (block, width), 1)
        at = ctx * tok + start - SIDE + col
        seen = (col - row >= 0) & (col - row < WINDOW) & (at >= 0) & (at < n_ctx * tok)
        s = jnp.where(seen, s, -1e30)
        e = jnp.exp(s - jnp.max(s, axis=1, keepdims=True))
        o = dot(e.astype(BF), vx[g, start : start + width])
        window = o / jnp.sum(e, axis=1, keepdims=True)
        heads[g, 0, rows] = (normed[rows] + window).astype(BF)
        y_copies[g, i] = [
            remote(heads.at[g, 0, rows], heads.at[g, d, rows], y_s.at[g, i, d], y_r.at[g, i, d], y_peer(d))
            for d in range(1, ys)
        ]

    forwards = []

    def forward_weights():
        for d in range(1, ys):
            w_copies[d - 1].wait_recv()
            forwards.append(remote(pw.at[d, my_half], pw.at[d, my_half], ws_s.at[d], ws_r.at[d], sib))

    def weights_here():
        load_p.wait()
        for c in forwards:
            c.wait_recv()

    sent = {}

    def project(g, i, which):
        rows = slice(i * block, (i + 1) * block)
        cols = pl.ds(pl.multiple_of(which * wide, wide), wide)
        t = dot(heads[g, 0, rows], pw[0, :, cols])
        for d in range(1, ys):
            t += dot(heads[g, d, rows], pw[d, :, cols])
        return t

    def project_other(g, i):
        for c in y_copies[g, i]:
            c.wait_recv()
        xs[g, i] = project(g, i, 1 - x_lo).astype(BF)
        sent[g, i] = remote(xs.at[g, i], xr.at[g, i], x_s.at[g, i], x_r.at[g, i], pair)

    def project_own(g, i):
        xa[g, i] = project(g, i, x_lo)

    def finish(g, i):
        sent[g, i].wait_recv()
        mixed_ref[g, i * block : (i + 1) * block] = (xa[g, i] + xr[g, i].astype(F32)).astype(BF)

    def nothing():
        pass

    def interleave(steps_of, others):
        others = list(others)
        for _ in steps_of:
            if others:
                others.pop(0)()
        for other in others:
            other()

    norms()
    gradients(0)
    load_q.wait()
    interleave(
        sum_gradients(0),
        [
            lambda: (send_far(0, (2,)), send_weights(1), hidden(0, 0)),
            lambda: hidden(0, 1),
            lambda: (send_far(0, (3,)), send_weights(2), fast_out()),
            nothing,
            lambda: send_weights(3),
            lambda: send_far(1, (0,)),
            lambda: attend(0, 0),
            lambda: (send_far(1, (1,)), attend(0, 1)),
            nothing,
        ],
    )
    forward_weights()
    send_far(1, (2, 3))
    update(0)
    gradients(1)
    interleave(
        sum_gradients(1),
        [
            lambda: (weights_here(), project_other(0, 0), project_other(0, 1)),
            lambda: (hidden(1, 0), hidden(1, 1), fast_out()),
            lambda: attend(1, 0),
            lambda: attend(1, 1),
            lambda: (norms(), project_own(0, 0)),
            lambda: project_own(0, 1),
            lambda: project_other(1, 0),
            lambda: project_other(1, 1),
            lambda: (project_own(1, 0), project_own(1, 1)),
        ],
    )
    update(1)
    for g in range(GROUPS):
        for i in range(CHUNKS):
            finish(g, i)
    for c in waiting:
        c.wait_send()


def local(query, key_in, value, rates, w_in, w_gate, w_out, norm_gain, proj_weight):
    tok = query.shape[1]
    zs = lax.axis_size("ctx") // 4
    ys = lax.axis_size("head") // 2
    piece = DH // zs + HALF // zs
    wide = proj_weight.shape[1] // (2 * ys)
    vmem = pl.BlockSpec(memory_space=pltpu.VMEM)
    hbm = pl.BlockSpec(memory_space=pl.ANY)
    dma = pltpu.SemaphoreType.DMA
    ext = tok + WINDOW
    chunk = (GROUPS, CHUNKS, tok // CHUNKS, wide)
    mixed, new1, new3, new2 = pl.pallas_call(
        functools.partial(kernel, zs, ys),
        out_shape=(
            jax.ShapeDtypeStruct((GROUPS, tok, wide), BF),
            jax.ShapeDtypeStruct((DH, HID), BF),
            jax.ShapeDtypeStruct((DH, HID), BF),
            jax.ShapeDtypeStruct((HID, DH), BF),
        ),
        in_specs=[hbm, hbm, hbm, vmem, vmem, vmem, vmem, vmem, hbm],
        out_specs=(vmem, vmem, vmem, vmem),
        scratch_shapes=[
            pltpu.VMEM((GROUPS, tok, DH), BF),
            pltpu.VMEM((GROUPS, ext, DH), BF),
            pltpu.VMEM((GROUPS, ext, DH), BF),
            pltpu.VMEM((GROUPS, tok), F32),
            pltpu.VMEM((2, DH, 2 * HALF), F32),
            pltpu.VMEM((HID, DH), F32),
            pltpu.VMEM((2, DH, 2 * HALF), BF),
            pltpu.VMEM((HID, DH), BF),
            pltpu.VMEM((2, 1, 2 * HALF), F32),
            pltpu.VMEM((1, DH), F32),
            pltpu.VMEM((DH, 2 * HALF), F32),
            pltpu.VMEM((HALF, DH), F32),
            pltpu.VMEM((tok, HID), BF),
            pltpu.VMEM((tok, DH), F32),
            pltpu.VMEM((GROUPS, zs, piece, DH), BF),
            pltpu.VMEM((GROUPS, 2, zs // 2, 2, piece // 2, DH), BF),
            pltpu.VMEM((GROUPS, 2, piece // 2, DH), BF),
            pltpu.VMEM((GROUPS, 2, piece // 2, DH), BF),
            pltpu.VMEM((GROUPS, 2, zs, piece, DH), BF),
            pltpu.VMEM((GROUPS, ys, tok, DH), BF),
            pltpu.VMEM((ys, DH, 2 * wide), BF),
            pltpu.VMEM(chunk, BF),
            pltpu.VMEM(chunk, BF),
            pltpu.VMEM(chunk, F32),
            dma((2 * GROUPS + 2,)),
            dma((2 * GROUPS + 1,)),
            dma((2 * GROUPS + 1,)),
            dma((GROUPS, 2, FAR_PARTS)),
            dma((GROUPS, 2, FAR_PARTS)),
            dma((GROUPS, 2, zs // 2, 2)),
            dma((GROUPS, 2, zs // 2, 2)),
            dma((GROUPS, 2)),
            dma((GROUPS, 2)),
            dma((GROUPS, 2, zs // 2, 2)),
            dma((GROUPS, 2, zs // 2, 2)),
            dma((GROUPS, zs, 2)),
            dma((GROUPS, zs, 2)),
            dma((ys,)),
            dma((ys,)),
            dma((ys,)),
            dma((ys,)),
            dma((GROUPS, CHUNKS, ys)),
            dma((GROUPS, CHUNKS, ys)),
            dma((GROUPS, CHUNKS)),
            dma((GROUPS, CHUNKS)),
        ],
        compiler_params=pltpu.CompilerParams(
            collective_id=0, has_side_effects=True, vmem_limit_bytes=60 * 1024 * 1024
        ),
    )(
        query,
        key_in,
        value,
        rates[:, 0],
        w_in[0],
        w_gate[0],
        w_out[0],
        norm_gain,
        proj_weight,
    )
    return mixed, new1[None], new3[None], new2[None]


def solution(mesh):
    return jax.shard_map(
        local,
        mesh=mesh,
        in_specs=(
            P(None, "ctx", "head"),
            P(None, "ctx", "head"),
            P(None, "ctx", "head"),
            P(None, "head", "ctx"),
            P("head", None, None),
            P("head", None, None),
            P("head", None, None),
            P("head", None),
            P("head", None),
        ),
        out_specs=(
            P(None, "ctx", "head"),
            P("head", None, None),
            P("head", None, None),
            P("head", None, None),
        ),
        check_vma=False,
    )
```

```python
import functools

import jax
import jax.numpy as jnp
from jax import lax
from jax.experimental import pallas as pl
from jax.experimental.pallas import tpu as pltpu
from jax.sharding import PartitionSpec as P

DH = 512
HID = 512
HALF = HID // 2
GROUPS = 2
WINDOW = 1024
SIDE = WINDOW // 2
A = DH**-0.5
B = HID**-0.5
CHUNKS = 2
FAR_PARTS = 4
BF = jnp.bfloat16
F32 = jnp.float32


def dot(x, y, dims=((1,), (0,))):
    return lax.dot_general(x, y, (dims, ((), ())), preferred_element_type=F32)


def kernel(
    zs,
    ys,
    q_hbm,
    k_hbm,
    v_hbm,
    rates_ref,
    w1_ref,
    w3_ref,
    w2_ref,
    gain_ref,
    proj_hbm,
    mixed_ref,
    out1_ref,
    out3_ref,
    out2_ref,
    qs,
    kx,
    vx,
    rx,
    s13,
    s2,
    b13,
    b2,
    kept13,
    kept2,
    acc13,
    acc2,
    hq,
    normed,
    part,
    landed,
    mine,
    theirs,
    gathered,
    heads,
    pw,
    xs,
    xr,
    xa,
    loc_sem,
    sib_s,
    sib_r,
    far_s,
    far_r,
    rs_s,
    rs_r,
    hi_s,
    hi_r,
    ag_s,
    ag_r,
    ex_s,
    ex_r,
    w_s,
    w_r,
    ws_s,
    ws_r,
    y_s,
    y_r,
    x_s,
    x_r,
):
    tok = kx.shape[1] - 2 * SIDE
    wide = xs.shape[-1]
    block = tok // CHUNKS
    rows13, rows2 = DH // zs, HALF // zs
    piece = rows13 + rows2
    ctx = lax.axis_index("ctx")
    head = lax.axis_index("head")
    n_ctx = 4 * zs
    core = lax.rem(ctx, 2)
    x_hi = lax.rem(lax.div(ctx, 2), 2)
    z = lax.div(ctx, 4)
    y = lax.div(head, 2)
    x_lo = lax.rem(head, 2)
    sib = (ctx + 1 - 2 * core, head)
    far = (lax.rem(ctx + 2 * core - 1 + n_ctx, n_ctx), head)
    pair = (ctx, head + 1 - 2 * x_lo)
    across = (ctx + 2 - 4 * x_hi, head)

    def z_at(d):
        return lax.rem(z + d + zs, zs)

    along = [(z_at(d) * 4 + x_hi * 2 + core, head) for d in (1, -1)]

    def y_peer(d):
        return (ctx, lax.rem(y + d, ys) * 2 + x_lo)

    peers = [sib, far, pair, across] + along + [y_peer(d) for d in range(1, ys)]

    def local_copy(src, dst, n):
        c = pltpu.make_async_copy(src, dst, loc_sem.at[n])
        c.start()
        return c

    waiting = []

    def remote(src, dst, send, recv, peer):
        c = pltpu.make_async_remote_copy(
            src_ref=src, dst_ref=dst, send_sem=send, recv_sem=recv, device_id=peer, device_id_type=pl.DeviceIdType.MESH
        )
        c.start()
        waiting.append(c)
        return c

    own = pl.ds(SIDE, tok)
    my_half = pl.ds(pl.multiple_of(core * HALF, HALF), HALF)

    loads_k = [local_copy(k_hbm.at[g], kx.at[g, own], g) for g in range(GROUPS)]
    loads_v = [local_copy(v_hbm.at[g], vx.at[g, own], GROUPS + g) for g in range(GROUPS)]
    load_q = local_copy(q_hbm, qs, 2 * GROUPS)
    load_p = local_copy(
        proj_hbm.at[:, pl.ds(pl.multiple_of(y * 2 * wide, 2 * wide), 2 * wide)], pw.at[0], 2 * GROUPS + 1
    )

    barrier = pltpu.get_barrier_semaphore()
    for peer in peers:
        pl.semaphore_signal(barrier, inc=1, device_id=peer, device_id_type=pl.DeviceIdType.MESH)
    def column_norm(x):
        return jnp.sqrt(jnp.sum(x * x, axis=0, keepdims=True))

    for c in range(2):
        cols = slice(c * HALF, (c + 1) * HALF)
        for j, w in enumerate((w1_ref, w3_ref)):
            into = slice(j * HALF, (j + 1) * HALF)
            b13[c, :, into] = w[:, cols]
            s13[c, :, into] = w[:, cols].astype(F32)
    b2[...] = w2_ref[...]
    s2[...] = w2_ref[...].astype(F32)

    def norms():
        for c in range(2):
            kept13[c] = column_norm(s13[c])
        kept2[...] = column_norm(s2[...])

    norms()
    pl.semaphore_wait(barrier, len(peers))

    to_sib = pl.ds(pl.multiple_of(core * WINDOW, SIDE), SIDE)
    from_sib = pl.ds(pl.multiple_of((1 - core) * WINDOW, SIDE), SIDE)

    def send_rows(g):
        return [
            remote(k_hbm.at[g], kx.at[g, to_sib], sib_s.at[2 * g], sib_r.at[2 * g], sib),
            remote(v_hbm.at[g], vx.at[g, to_sib], sib_s.at[2 * g + 1], sib_r.at[2 * g + 1], sib),
        ]

    far_copies = [[], []]
    far_rows = tok // FAR_PARTS

    def send_far(g, parts):
        for n in parts:
            rows = pl.ds(pl.multiple_of((1 - core) * WINDOW + n * far_rows, far_rows), far_rows)
            for j, (src, dst) in enumerate(((k_hbm, kx), (v_hbm, vx))):
                far_copies[g].append(
                    remote(
                        src.at[g, n * far_rows : (n + 1) * far_rows],
                        dst.at[g, rows],
                        far_s.at[g, j, n],
                        far_r.at[g, j, n],
                        far,
                    )
                )

    rate_copy = remote(rates_ref, rx, sib_s.at[2 * GROUPS], sib_r.at[2 * GROUPS], sib)
    sib_copies = [send_rows(0)]
    send_far(0, (0, 1))
    sib_copies.append(send_rows(1))
    w_copies = []

    def send_weights(d):
        cols = pl.ds(pl.multiple_of(lax.rem(y + d, ys) * 2 * wide, 2 * wide), 2 * wide)
        w_copies.append(remote(proj_hbm.at[my_half, cols], pw.at[d, my_half], w_s.at[d], w_r.at[d], y_peer(d)))

    def key_part(g, rows, rate_row, first):
        k = kx[g, rows]
        v = vx[g, rows]
        f = dot(k, b13[core]) * A
        f1, f3 = f[:, :HALF], f[:, HALF:]
        sig = jax.nn.sigmoid(f1)
        act = f1 * sig
        slope = sig * (1.0 + f1 * (1.0 - sig))
        hk = (act * f3).astype(BF)
        rate = jnp.transpose(jnp.broadcast_to(rate_row, (128, tok)))[:, :1]
        scaled = (v.astype(F32) * rate).astype(BF)
        back = dot(scaled, b2[my_half], ((1,), (1,))) * -B
        d13 = jnp.concatenate([(back * f3 * slope).astype(BF), (back * act).astype(BF)], axis=1)
        g2 = dot(hk, scaled, ((0,), (0,))) * -B
        g13 = dot(k, d13, ((0,), (0,))) * A
        if first:
            acc13[...] = g13
            acc2[...] = g2
        else:
            part[g, :, :rows13] = (acc13[...] + g13).reshape(zs, rows13, 2 * HALF).astype(BF)
            part[g, :, rows13:] = (acc2[...] + g2).reshape(zs, rows2, DH).astype(BF)

    def gradients(g):
        if g == 0:
            loads_k[0].wait()
            loads_v[0].wait()
        else:
            arrived(1)
        key_part(g, own, rates_ref[g : g + 1], True)
        if g == 0:
            rate_copy.wait_recv()
            for c in sib_copies[0]:
                c.wait_recv()
        key_part(g, from_sib, rx[g : g + 1], False)

    sub = piece // 2
    steps = zs // 2
    flows = ((0, 0), (1, 1), (0, 1), (1, 0))

    def rows_of(h):
        return pl.ds(h * sub, sub)

    def sum_gradients(g):
        last = {}
        for s in range(1, steps + 1):
            now = {}
            for way, h in flows:
                if s == 1 and way != h:
                    continue
                target = z_at((steps + 1 - s) * (1 - 2 * way))
                if (way, h) in last:
                    last[way, h].wait_recv()
                    got = landed[g, way, s - 2, h].astype(F32) + part[g, target, rows_of(h)].astype(F32)
                    landed[g, way, s - 2, h] = got.astype(BF)
                    src = landed.at[g, way, s - 2, h]
                else:
                    src = part.at[g, target, rows_of(h)]
                now[way, h] = remote(
                    src, landed.at[g, way, s - 1, h], rs_s.at[g, way, s - 1, h], rs_r.at[g, way, s - 1, h], along[way]
                )
            last = now
            yield
        swaps = []
        for h in range(2):
            for way in range(2):
                last[way, h].wait_recv()
            got = landed[g, 0, steps - 1, h].astype(F32) + landed[g, 1, steps - 1, h].astype(F32)
            mine[g, h] = (got + part[g, z, rows_of(h)].astype(F32)).astype(BF)
            swaps.append(remote(mine.at[g, h], theirs.at[g, h], hi_s.at[g, h], hi_r.at[g, h], across))
        yield
        exchanged = []

        def to_sibling(origin, h, n):
            at = gathered.at[g, core, origin, rows_of(h)]
            exchanged.append(remote(at, at, ex_s.at[g, n, h], ex_r.at[g, n, h], sib))

        last = {}
        for h in range(2):
            swaps[h].wait_recv()
            gathered[g, core, z, rows_of(h)] = (mine[g, h].astype(F32) + theirs[g, h].astype(F32)).astype(BF)
            for way in range(2):
                at = gathered.at[g, core, z, rows_of(h)]
                last[way, h] = remote(at, at, ag_s.at[g, way, 0, h], ag_r.at[g, way, 0, h], along[way])
            to_sibling(z, h, 0)
        yield
        for s in range(2, steps + 1):
            now = {}
            for way, h in flows:
                last[way, h].wait_recv()
                origin = z_at((s - 1) * (2 * way - 1))
                if s < steps or way == h:
                    at = gathered.at[g, core, origin, rows_of(h)]
                    now[way, h] = remote(
                        at, at, ag_s.at[g, way, s - 1, h], ag_r.at[g, way, s - 1, h], along[way]
                    )
                to_sibling(origin, h, 2 * (s - 1) - 1 + way)
            last = now
            yield
        for way in range(2):
            last[way, way].wait_recv()
            to_sibling(z_at(steps), way, zs - 1)
        for c in exchanged:
            c.wait_recv()

    def rescaled(before, grad, kept):
        changed = before - grad
        return changed * (kept / jnp.sqrt(jnp.sum(changed * changed, axis=0, keepdims=True) + 1e-6))

    def new13(g, c):
        grad = gathered[g, c, :, :rows13].astype(F32).reshape(DH, 2 * HALF)
        return rescaled(s13[c], grad, kept13[c])

    def new2(g):
        grad = gathered[g, :, :, rows13:].astype(F32).reshape(HID, DH)
        return rescaled(s2[...], grad, kept2[...])

    def update13(c):
        new = new13(0, c)
        s13[c] = new
        b13[c] = new.astype(BF)

    def update2():
        new = new2(0)
        s2[...] = new
        b2[...] = new.astype(BF)

    def last_update():
        for c in range(2):
            new = new13(1, c)
            out1_ref[:, c * HALF : (c + 1) * HALF] = new[:, :HALF].astype(BF)
            out3_ref[:, c * HALF : (c + 1) * HALF] = new[:, HALF:].astype(BF)
        out2_ref[...] = new2(1).astype(BF)

    done = set()

    def arrived(g):
        if g not in done:
            done.add(g)
            loads_k[g].wait()
            loads_v[g].wait()
            for c in sib_copies[g]:
                c.wait_recv()

    def hidden(g, c):
        f = dot(qs[g], b13[c]) * A
        f1 = f[:, :HALF]
        hq[:, c * HALF : (c + 1) * HALF] = (f1 * jax.nn.sigmoid(f1) * f[:, HALF:]).astype(BF)

    def fast_out():
        t = dot(hq[...], b2[...]) * B
        normed[...] = t * lax.rsqrt(jnp.mean(t * t, axis=1, keepdims=True) + 1e-6) * gain_ref[...]

    width = block + WINDOW
    y_copies = {}

    def attend(g, i):
        if i == 0:
            for c in far_copies[g]:
                c.wait_recv()
        start = i * block
        rows = slice(start, start + block)
        s = dot(qs[g, rows], kx[g, start : start + width], ((1,), (1,))) * A
        row = lax.broadcasted_iota(jnp.int32, (block, width), 0)
        col = lax.broadcasted_iota(jnp.int32, (block, width), 1)
        at = ctx * tok + start - SIDE + col
        seen = (col - row >= 0) & (col - row < WINDOW) & (at >= 0) & (at < n_ctx * tok)
        s = jnp.where(seen, s, -1e30)
        e = jnp.exp(s - jnp.max(s, axis=1, keepdims=True))
        o = dot(e.astype(BF), vx[g, start : start + width])
        window = o / jnp.sum(e, axis=1, keepdims=True)
        heads[g, 0, rows] = (normed[rows] + window).astype(BF)
        y_copies[g, i] = [
            remote(heads.at[g, 0, rows], heads.at[g, d, rows], y_s.at[g, i, d], y_r.at[g, i, d], y_peer(d))
            for d in range(1, ys)
        ]

    forwards = []

    def forward_weights():
        for d in range(1, ys):
            w_copies[d - 1].wait_recv()
            forwards.append(remote(pw.at[d, my_half], pw.at[d, my_half], ws_s.at[d], ws_r.at[d], sib))

    def weights_here():
        load_p.wait()
        for c in forwards:
            c.wait_recv()

    sent = {}

    def project(g, i, which):
        rows = slice(i * block, (i + 1) * block)
        cols = pl.ds(pl.multiple_of(which * wide, wide), wide)
        t = dot(heads[g, 0, rows], pw[0, :, cols])
        for d in range(1, ys):
            t += dot(heads[g, d, rows], pw[d, :, cols])
        return t

    def project_other(g, i):
        for c in y_copies[g, i]:
            c.wait_recv()
        xs[g, i] = project(g, i, 1 - x_lo).astype(BF)
        sent[g, i] = remote(xs.at[g, i], xr.at[g, i], x_s.at[g, i], x_r.at[g, i], pair)

    def project_own(g, i):
        xa[g, i] = project(g, i, x_lo)

    def finish(g, i):
        sent[g, i].wait_recv()
        mixed_ref[g, i * block : (i + 1) * block] = (xa[g, i] + xr[g, i].astype(F32)).astype(BF)

    def nothing():
        pass

    def interleave(steps_of, others):
        others = list(others)
        for _ in steps_of:
            if others:
                others.pop(0)()
        for other in others:
            other()

    for d in range(1, ys):
        send_weights(d)
    gradients(0)
    load_q.wait()
    interleave(
        sum_gradients(0),
        [
            lambda: (send_far(0, (2, 3)), hidden(0, 0)),
            lambda: (hidden(0, 1), fast_out()),
            nothing,
            nothing,
            lambda: attend(0, 0),
            lambda: (send_far(1, (0,)), attend(0, 1)),
            lambda: send_far(1, (1,)),
            lambda: (forward_weights(), send_far(1, (2, 3))),
            lambda: (weights_here(), project_other(0, 0)),
        ],
    )
    update13(core)
    update2()
    gradients(1)
    interleave(
        sum_gradients(1),
        [
            lambda: (update13(1 - core), hidden(1, 0), hidden(1, 1), fast_out(), attend(1, 0)),
            lambda: attend(1, 1),
            lambda: project_other(0, 1),
            lambda: (norms(), project_own(0, 0)),
            lambda: project_own(0, 1),
            lambda: project_other(1, 0),
            lambda: project_other(1, 1),
            nothing,
            lambda: (project_own(1, 0), project_own(1, 1)),
        ],
    )
    last_update()
    for g in range(GROUPS):
        for i in range(CHUNKS):
            finish(g, i)
    for c in waiting:
        c.wait_send()


def local(query, key_in, value, rates, w_in, w_gate, w_out, norm_gain, proj_weight):
    tok = query.shape[1]
    zs = lax.axis_size("ctx") // 4
    ys = lax.axis_size("head") // 2
    piece = DH // zs + HALF // zs
    wide = proj_weight.shape[1] // (2 * ys)
    vmem = pl.BlockSpec(memory_space=pltpu.VMEM)
    hbm = pl.BlockSpec(memory_space=pl.ANY)
    dma = pltpu.SemaphoreType.DMA
    ext = tok + WINDOW
    chunk = (GROUPS, CHUNKS, tok // CHUNKS, wide)
    mixed, new1, new3, new2 = pl.pallas_call(
        functools.partial(kernel, zs, ys),
        out_shape=(
            jax.ShapeDtypeStruct((GROUPS, tok, wide), BF),
            jax.ShapeDtypeStruct((DH, HID), BF),
            jax.ShapeDtypeStruct((DH, HID), BF),
            jax.ShapeDtypeStruct((HID, DH), BF),
        ),
        in_specs=[hbm, hbm, hbm, vmem, vmem, vmem, vmem, vmem, hbm],
        out_specs=(vmem, vmem, vmem, vmem),
        scratch_shapes=[
            pltpu.VMEM((GROUPS, tok, DH), BF),
            pltpu.VMEM((GROUPS, ext, DH), BF),
            pltpu.VMEM((GROUPS, ext, DH), BF),
            pltpu.VMEM((GROUPS, tok), F32),
            pltpu.VMEM((2, DH, 2 * HALF), F32),
            pltpu.VMEM((HID, DH), F32),
            pltpu.VMEM((2, DH, 2 * HALF), BF),
            pltpu.VMEM((HID, DH), BF),
            pltpu.VMEM((2, 1, 2 * HALF), F32),
            pltpu.VMEM((1, DH), F32),
            pltpu.VMEM((DH, 2 * HALF), F32),
            pltpu.VMEM((HALF, DH), F32),
            pltpu.VMEM((tok, HID), BF),
            pltpu.VMEM((tok, DH), F32),
            pltpu.VMEM((GROUPS, zs, piece, DH), BF),
            pltpu.VMEM((GROUPS, 2, zs // 2, 2, piece // 2, DH), BF),
            pltpu.VMEM((GROUPS, 2, piece // 2, DH), BF),
            pltpu.VMEM((GROUPS, 2, piece // 2, DH), BF),
            pltpu.VMEM((GROUPS, 2, zs, piece, DH), BF),
            pltpu.VMEM((GROUPS, ys, tok, DH), BF),
            pltpu.VMEM((ys, DH, 2 * wide), BF),
            pltpu.VMEM(chunk, BF),
            pltpu.VMEM(chunk, BF),
            pltpu.VMEM(chunk, F32),
            dma((2 * GROUPS + 2,)),
            dma((2 * GROUPS + 1,)),
            dma((2 * GROUPS + 1,)),
            dma((GROUPS, 2, FAR_PARTS)),
            dma((GROUPS, 2, FAR_PARTS)),
            dma((GROUPS, 2, zs // 2, 2)),
            dma((GROUPS, 2, zs // 2, 2)),
            dma((GROUPS, 2)),
            dma((GROUPS, 2)),
            dma((GROUPS, 2, zs // 2, 2)),
            dma((GROUPS, 2, zs // 2, 2)),
            dma((GROUPS, zs, 2)),
            dma((GROUPS, zs, 2)),
            dma((ys,)),
            dma((ys,)),
            dma((ys,)),
            dma((ys,)),
            dma((GROUPS, CHUNKS, ys)),
            dma((GROUPS, CHUNKS, ys)),
            dma((GROUPS, CHUNKS)),
            dma((GROUPS, CHUNKS)),
        ],
        compiler_params=pltpu.CompilerParams(
            collective_id=0, has_side_effects=True, vmem_limit_bytes=60 * 1024 * 1024
        ),
    )(
        query,
        key_in,
        value,
        rates[:, 0],
        w_in[0],
        w_gate[0],
        w_out[0],
        norm_gain,
        proj_weight,
    )
    return mixed, new1[None], new3[None], new2[None]


def solution(mesh):
    return jax.shard_map(
        local,
        mesh=mesh,
        in_specs=(
            P(None, "ctx", "head"),
            P(None, "ctx", "head"),
            P(None, "ctx", "head"),
            P(None, "head", "ctx"),
            P("head", None, None),
            P("head", None, None),
            P("head", None, None),
            P("head", None),
            P("head", None),
        ),
        out_specs=(
            P(None, "ctx", "head"),
            P("head", None, None),
            P("head", None, None),
            P("head", None, None),
        ),
        check_vma=False,
    )
```

```python
import functools

import jax
import jax.numpy as jnp
from jax import lax
from jax.experimental import pallas as pl
from jax.experimental.pallas import tpu as pltpu
from jax.sharding import PartitionSpec as P

DH = 512
HID = 512
HALF = HID // 2
GROUPS = 2
WINDOW = 1024
SIDE = WINDOW // 2
A = DH**-0.5
B = HID**-0.5
CHUNKS = 2
FAR_PARTS = 4
BF = jnp.bfloat16
F32 = jnp.float32


def dot(x, y, dims=((1,), (0,))):
    return lax.dot_general(x, y, (dims, ((), ())), preferred_element_type=F32)


def kernel(
    zs,
    ys,
    q_hbm,
    k_hbm,
    v_hbm,
    rates_ref,
    w1_ref,
    w3_ref,
    w2_ref,
    gain_ref,
    proj_hbm,
    mixed_ref,
    out1_ref,
    out3_ref,
    out2_ref,
    qs,
    kx,
    vx,
    rx,
    s13,
    s2,
    b13,
    b2,
    kept13,
    kept2,
    acc13,
    acc2,
    hq,
    normed,
    part,
    landed,
    mine,
    theirs,
    gathered,
    heads,
    pw,
    xs,
    xr,
    xa,
    loc_sem,
    sib_s,
    sib_r,
    far_s,
    far_r,
    rs_s,
    rs_r,
    hi_s,
    hi_r,
    ag_s,
    ag_r,
    ex_s,
    ex_r,
    w_s,
    w_r,
    ws_s,
    ws_r,
    y_s,
    y_r,
    x_s,
    x_r,
):
    tok = kx.shape[1] - 2 * SIDE
    wide = xs.shape[-1]
    block = tok // CHUNKS
    rows13, rows2 = DH // zs, HALF // zs
    piece = rows13 + rows2
    ctx = lax.axis_index("ctx")
    head = lax.axis_index("head")
    n_ctx = 4 * zs
    core = lax.rem(ctx, 2)
    x_hi = lax.rem(lax.div(ctx, 2), 2)
    z = lax.div(ctx, 4)
    y = lax.div(head, 2)
    x_lo = lax.rem(head, 2)
    sib = (ctx + 1 - 2 * core, head)
    far = (lax.rem(ctx + 2 * core - 1 + n_ctx, n_ctx), head)
    pair = (ctx, head + 1 - 2 * x_lo)
    across = (ctx + 2 - 4 * x_hi, head)

    def z_at(d):
        return lax.rem(z + d + zs, zs)

    along = [(z_at(d) * 4 + x_hi * 2 + core, head) for d in (1, -1)]

    def y_peer(d):
        return (ctx, lax.rem(y + d, ys) * 2 + x_lo)

    peers = [sib, far, pair, across] + along + [y_peer(d) for d in range(1, ys)]

    def local_copy(src, dst, n):
        c = pltpu.make_async_copy(src, dst, loc_sem.at[n])
        c.start()
        return c

    waiting = []

    def remote(src, dst, send, recv, peer):
        c = pltpu.make_async_remote_copy(
            src_ref=src, dst_ref=dst, send_sem=send, recv_sem=recv, device_id=peer, device_id_type=pl.DeviceIdType.MESH
        )
        c.start()
        waiting.append(c)
        return c

    own = pl.ds(SIDE, tok)
    my_half = pl.ds(pl.multiple_of(core * HALF, HALF), HALF)

    loads_k = [local_copy(k_hbm.at[g], kx.at[g, own], g) for g in range(GROUPS)]
    loads_v = [local_copy(v_hbm.at[g], vx.at[g, own], GROUPS + g) for g in range(GROUPS)]
    load_q = local_copy(q_hbm, qs, 2 * GROUPS)
    load_p = local_copy(
        proj_hbm.at[:, pl.ds(pl.multiple_of(y * 2 * wide, 2 * wide), 2 * wide)], pw.at[0], 2 * GROUPS + 1
    )

    barrier = pltpu.get_barrier_semaphore()
    for peer in peers:
        pl.semaphore_signal(barrier, inc=1, device_id=peer, device_id_type=pl.DeviceIdType.MESH)
    def column_norm(x):
        return jnp.sqrt(jnp.sum(x * x, axis=0, keepdims=True))

    for c in range(2):
        cols = slice(c * HALF, (c + 1) * HALF)
        for j, w in enumerate((w1_ref, w3_ref)):
            into = slice(j * HALF, (j + 1) * HALF)
            b13[c, :, into] = w[:, cols]
            s13[c, :, into] = w[:, cols].astype(F32)
    b2[...] = w2_ref[...]
    s2[...] = w2_ref[...].astype(F32)

    def norms():
        for c in range(2):
            kept13[c] = column_norm(s13[c])
        kept2[...] = column_norm(s2[...])

    norms()
    pl.semaphore_wait(barrier, len(peers))

    to_sib = pl.ds(pl.multiple_of(core * WINDOW, SIDE), SIDE)
    from_sib = pl.ds(pl.multiple_of((1 - core) * WINDOW, SIDE), SIDE)

    def send_rows(g):
        return [
            remote(k_hbm.at[g], kx.at[g, to_sib], sib_s.at[2 * g], sib_r.at[2 * g], sib),
            remote(v_hbm.at[g], vx.at[g, to_sib], sib_s.at[2 * g + 1], sib_r.at[2 * g + 1], sib),
        ]

    far_copies = [[], []]
    far_rows = tok // FAR_PARTS

    def send_far(g, parts):
        for n in parts:
            rows = pl.ds(pl.multiple_of((1 - core) * WINDOW + n * far_rows, far_rows), far_rows)
            for j, (src, dst) in enumerate(((k_hbm, kx), (v_hbm, vx))):
                far_copies[g].append(
                    remote(
                        src.at[g, n * far_rows : (n + 1) * far_rows],
                        dst.at[g, rows],
                        far_s.at[g, j, n],
                        far_r.at[g, j, n],
                        far,
                    )
                )

    rate_copy = remote(rates_ref, rx, sib_s.at[2 * GROUPS], sib_r.at[2 * GROUPS], sib)
    sib_copies = [send_rows(0)]
    send_far(0, (0, 1))
    sib_copies.append(send_rows(1))
    w_copies = []

    def send_weights(d):
        cols = pl.ds(pl.multiple_of(lax.rem(y + d, ys) * 2 * wide, 2 * wide), 2 * wide)
        w_copies.append(remote(proj_hbm.at[my_half, cols], pw.at[d, my_half], w_s.at[d], w_r.at[d], y_peer(d)))

    def key_part(g, rows, rate_row, first):
        k = kx[g, rows]
        v = vx[g, rows]
        f = dot(k, b13[core]) * A
        f1, f3 = f[:, :HALF], f[:, HALF:]
        sig = jax.nn.sigmoid(f1)
        act = f1 * sig
        slope = sig * (1.0 + f1 * (1.0 - sig))
        hk = (act * f3).astype(BF)
        rate = jnp.transpose(jnp.broadcast_to(rate_row, (128, tok)))[:, :1]
        scaled = (v.astype(F32) * rate).astype(BF)
        back = dot(scaled, b2[my_half], ((1,), (1,))) * -B
        d13 = jnp.concatenate([(back * f3 * slope).astype(BF), (back * act).astype(BF)], axis=1)
        g2 = dot(hk, scaled, ((0,), (0,))) * -B
        g13 = dot(k, d13, ((0,), (0,))) * A
        if first:
            acc13[...] = g13
            acc2[...] = g2
        else:
            part[g, :, :rows13] = (acc13[...] + g13).reshape(zs, rows13, 2 * HALF).astype(BF)
            part[g, :, rows13:] = (acc2[...] + g2).reshape(zs, rows2, DH).astype(BF)

    def gradients(g):
        if g == 0:
            loads_k[0].wait()
            loads_v[0].wait()
        else:
            arrived(1)
        key_part(g, own, rates_ref[g : g + 1], True)
        if g == 0:
            rate_copy.wait_recv()
            for c in sib_copies[0]:
                c.wait_recv()
        key_part(g, from_sib, rx[g : g + 1], False)

    sub = piece // 2
    steps = zs // 2
    flows = ((0, 0), (1, 1), (0, 1), (1, 0))

    def rows_of(h):
        return pl.ds(h * sub, sub)

    def sum_gradients(g):
        last = {}
        for s in range(1, steps + 1):
            now = {}
            for way, h in flows:
                if s == 1 and way != h:
                    continue
                target = z_at((steps + 1 - s) * (1 - 2 * way))
                if (way, h) in last:
                    last[way, h].wait_recv()
                    got = landed[g, way, s - 2, h].astype(F32) + part[g, target, rows_of(h)].astype(F32)
                    landed[g, way, s - 2, h] = got.astype(BF)
                    src = landed.at[g, way, s - 2, h]
                else:
                    src = part.at[g, target, rows_of(h)]
                now[way, h] = remote(
                    src, landed.at[g, way, s - 1, h], rs_s.at[g, way, s - 1, h], rs_r.at[g, way, s - 1, h], along[way]
                )
            last = now
            yield
        swaps = []
        for h in range(2):
            for way in range(2):
                last[way, h].wait_recv()
            got = landed[g, 0, steps - 1, h].astype(F32) + landed[g, 1, steps - 1, h].astype(F32)
            mine[g, h] = (got + part[g, z, rows_of(h)].astype(F32)).astype(BF)
            swaps.append(remote(mine.at[g, h], theirs.at[g, h], hi_s.at[g, h], hi_r.at[g, h], across))
        yield
        exchanged = []

        def to_sibling(origin, h, n):
            at = gathered.at[g, core, origin, rows_of(h)]
            exchanged.append(remote(at, at, ex_s.at[g, n, h], ex_r.at[g, n, h], sib))

        last = {}
        for h in range(2):
            swaps[h].wait_recv()
            gathered[g, core, z, rows_of(h)] = (mine[g, h].astype(F32) + theirs[g, h].astype(F32)).astype(BF)
            for way in range(2):
                at = gathered.at[g, core, z, rows_of(h)]
                last[way, h] = remote(at, at, ag_s.at[g, way, 0, h], ag_r.at[g, way, 0, h], along[way])
            to_sibling(z, h, 0)
        yield
        for s in range(2, steps + 1):
            now = {}
            for way, h in flows:
                last[way, h].wait_recv()
                origin = z_at((s - 1) * (2 * way - 1))
                if s < steps or way == h:
                    at = gathered.at[g, core, origin, rows_of(h)]
                    now[way, h] = remote(
                        at, at, ag_s.at[g, way, s - 1, h], ag_r.at[g, way, s - 1, h], along[way]
                    )
                to_sibling(origin, h, 2 * (s - 1) - 1 + way)
            last = now
            yield
        for way in range(2):
            last[way, way].wait_recv()
            to_sibling(z_at(steps), way, zs - 1)
        for c in exchanged:
            c.wait_recv()

    def rescaled(before, grad, kept):
        changed = before - grad
        return changed * (kept / jnp.sqrt(jnp.sum(changed * changed, axis=0, keepdims=True) + 1e-6))

    def new13(g, c):
        grad = gathered[g, c, :, :rows13].astype(F32).reshape(DH, 2 * HALF)
        return rescaled(s13[c], grad, kept13[c])

    def new2(g):
        grad = gathered[g, :, :, rows13:].astype(F32).reshape(HID, DH)
        return rescaled(s2[...], grad, kept2[...])

    def update13(c):
        new = new13(0, c)
        s13[c] = new
        b13[c] = new.astype(BF)

    def update2():
        new = new2(0)
        s2[...] = new
        b2[...] = new.astype(BF)

    def last_update():
        for c in range(2):
            new = new13(1, c)
            out1_ref[:, c * HALF : (c + 1) * HALF] = new[:, :HALF].astype(BF)
            out3_ref[:, c * HALF : (c + 1) * HALF] = new[:, HALF:].astype(BF)
        out2_ref[...] = new2(1).astype(BF)

    done = set()

    def arrived(g):
        if g not in done:
            done.add(g)
            loads_k[g].wait()
            loads_v[g].wait()
            for c in sib_copies[g]:
                c.wait_recv()

    def hidden(g, c):
        f = dot(qs[g], b13[c]) * A
        f1 = f[:, :HALF]
        hq[:, c * HALF : (c + 1) * HALF] = (f1 * jax.nn.sigmoid(f1) * f[:, HALF:]).astype(BF)

    def fast_out():
        t = dot(hq[...], b2[...]) * B
        normed[...] = t * lax.rsqrt(jnp.mean(t * t, axis=1, keepdims=True) + 1e-6) * gain_ref[...]

    width = block + WINDOW
    y_copies = {}

    def attend(g, i):
        if i == 0:
            for c in far_copies[g]:
                c.wait_recv()
        start = i * block
        rows = slice(start, start + block)
        s = dot(qs[g, rows], kx[g, start : start + width], ((1,), (1,))) * A
        row = lax.broadcasted_iota(jnp.int32, (block, width), 0)
        col = lax.broadcasted_iota(jnp.int32, (block, width), 1)
        at = ctx * tok + start - SIDE + col
        seen = (col - row >= 0) & (col - row < WINDOW) & (at >= 0) & (at < n_ctx * tok)
        s = jnp.where(seen, s, -1e30)
        e = jnp.exp(s - jnp.max(s, axis=1, keepdims=True))
        o = dot(e.astype(BF), vx[g, start : start + width])
        window = o / jnp.sum(e, axis=1, keepdims=True)
        heads[g, 0, rows] = (normed[rows] + window).astype(BF)
        y_copies[g, i] = [
            remote(heads.at[g, 0, rows], heads.at[g, d, rows], y_s.at[g, i, d], y_r.at[g, i, d], y_peer(d))
            for d in range(1, ys)
        ]

    forwards = []

    def forward_weights():
        for d in range(1, ys):
            w_copies[d - 1].wait_recv()
            forwards.append(remote(pw.at[d, my_half], pw.at[d, my_half], ws_s.at[d], ws_r.at[d], sib))

    def weights_here():
        load_p.wait()
        for c in forwards:
            c.wait_recv()

    sent = {}

    def project(g, i, which):
        rows = slice(i * block, (i + 1) * block)
        cols = pl.ds(pl.multiple_of(which * wide, wide), wide)
        t = dot(heads[g, 0, rows], pw[0, :, cols])
        for d in range(1, ys):
            t += dot(heads[g, d, rows], pw[d, :, cols])
        return t

    def project_other(g, i):
        for c in y_copies[g, i]:
            c.wait_recv()
        xs[g, i] = project(g, i, 1 - x_lo).astype(BF)
        sent[g, i] = remote(xs.at[g, i], xr.at[g, i], x_s.at[g, i], x_r.at[g, i], pair)

    def project_own(g, i):
        xa[g, i] = project(g, i, x_lo)

    def finish(g, i):
        sent[g, i].wait_recv()
        mixed_ref[g, i * block : (i + 1) * block] = (xa[g, i] + xr[g, i].astype(F32)).astype(BF)

    def nothing():
        pass

    def interleave(steps_of, others):
        others = list(others)
        for _ in steps_of:
            if others:
                others.pop(0)()
        for other in others:
            other()

    for d in range(1, ys):
        send_weights(d)
    gradients(0)
    load_q.wait()
    interleave(
        sum_gradients(0),
        [
            lambda: (send_far(0, (2,)), hidden(0, 0)),
            lambda: (send_far(0, (3,)), hidden(0, 1), fast_out()),
            nothing,
            nothing,
            lambda: attend(0, 0),
            lambda: (send_far(1, (0,)), attend(0, 1)),
            lambda: send_far(1, (1,)),
            lambda: (forward_weights(), send_far(1, (2, 3))),
            lambda: (weights_here(), project_other(0, 0)),
        ],
    )
    update13(core)
    update2()
    gradients(1)
    interleave(
        sum_gradients(1),
        [
            lambda: (update13(1 - core), hidden(1, 0), hidden(1, 1), fast_out(), attend(1, 0)),
            lambda: attend(1, 1),
            lambda: project_other(0, 1),
            lambda: (norms(), project_own(0, 0)),
            lambda: project_own(0, 1),
            lambda: project_other(1, 0),
            lambda: project_other(1, 1),
            nothing,
            lambda: (project_own(1, 0), project_own(1, 1)),
        ],
    )
    last_update()
    for g in range(GROUPS):
        for i in range(CHUNKS):
            finish(g, i)
    for c in waiting:
        c.wait_send()


def local(query, key_in, value, rates, w_in, w_gate, w_out, norm_gain, proj_weight):
    tok = query.shape[1]
    zs = lax.axis_size("ctx") // 4
    ys = lax.axis_size("head") // 2
    piece = DH // zs + HALF // zs
    wide = proj_weight.shape[1] // (2 * ys)
    vmem = pl.BlockSpec(memory_space=pltpu.VMEM)
    hbm = pl.BlockSpec(memory_space=pl.ANY)
    dma = pltpu.SemaphoreType.DMA
    ext = tok + WINDOW
    chunk = (GROUPS, CHUNKS, tok // CHUNKS, wide)
    mixed, new1, new3, new2 = pl.pallas_call(
        functools.partial(kernel, zs, ys),
        out_shape=(
            jax.ShapeDtypeStruct((GROUPS, tok, wide), BF),
            jax.ShapeDtypeStruct((DH, HID), BF),
            jax.ShapeDtypeStruct((DH, HID), BF),
            jax.ShapeDtypeStruct((HID, DH), BF),
        ),
        in_specs=[hbm, hbm, hbm, vmem, vmem, vmem, vmem, vmem, hbm],
        out_specs=(vmem, vmem, vmem, vmem),
        scratch_shapes=[
            pltpu.VMEM((GROUPS, tok, DH), BF),
            pltpu.VMEM((GROUPS, ext, DH), BF),
            pltpu.VMEM((GROUPS, ext, DH), BF),
            pltpu.VMEM((GROUPS, tok), F32),
            pltpu.VMEM((2, DH, 2 * HALF), F32),
            pltpu.VMEM((HID, DH), F32),
            pltpu.VMEM((2, DH, 2 * HALF), BF),
            pltpu.VMEM((HID, DH), BF),
            pltpu.VMEM((2, 1, 2 * HALF), F32),
            pltpu.VMEM((1, DH), F32),
            pltpu.VMEM((DH, 2 * HALF), F32),
            pltpu.VMEM((HALF, DH), F32),
            pltpu.VMEM((tok, HID), BF),
            pltpu.VMEM((tok, DH), F32),
            pltpu.VMEM((GROUPS, zs, piece, DH), BF),
            pltpu.VMEM((GROUPS, 2, zs // 2, 2, piece // 2, DH), BF),
            pltpu.VMEM((GROUPS, 2, piece // 2, DH), BF),
            pltpu.VMEM((GROUPS, 2, piece // 2, DH), BF),
            pltpu.VMEM((GROUPS, 2, zs, piece, DH), BF),
            pltpu.VMEM((GROUPS, ys, tok, DH), BF),
            pltpu.VMEM((ys, DH, 2 * wide), BF),
            pltpu.VMEM(chunk, BF),
            pltpu.VMEM(chunk, BF),
            pltpu.VMEM(chunk, F32),
            dma((2 * GROUPS + 2,)),
            dma((2 * GROUPS + 1,)),
            dma((2 * GROUPS + 1,)),
            dma((GROUPS, 2, FAR_PARTS)),
            dma((GROUPS, 2, FAR_PARTS)),
            dma((GROUPS, 2, zs // 2, 2)),
            dma((GROUPS, 2, zs // 2, 2)),
            dma((GROUPS, 2)),
            dma((GROUPS, 2)),
            dma((GROUPS, 2, zs // 2, 2)),
            dma((GROUPS, 2, zs // 2, 2)),
            dma((GROUPS, zs, 2)),
            dma((GROUPS, zs, 2)),
            dma((ys,)),
            dma((ys,)),
            dma((ys,)),
            dma((ys,)),
            dma((GROUPS, CHUNKS, ys)),
            dma((GROUPS, CHUNKS, ys)),
            dma((GROUPS, CHUNKS)),
            dma((GROUPS, CHUNKS)),
        ],
        compiler_params=pltpu.CompilerParams(
            collective_id=0, has_side_effects=True, vmem_limit_bytes=60 * 1024 * 1024
        ),
    )(
        query,
        key_in,
        value,
        rates[:, 0],
        w_in[0],
        w_gate[0],
        w_out[0],
        norm_gain,
        proj_weight,
    )
    return mixed, new1[None], new3[None], new2[None]


def solution(mesh):
    return jax.shard_map(
        local,
        mesh=mesh,
        in_specs=(
            P(None, "ctx", "head"),
            P(None, "ctx", "head"),
            P(None, "ctx", "head"),
            P(None, "head", "ctx"),
            P("head", None, None),
            P("head", None, None),
            P("head", None, None),
            P("head", None),
            P("head", None),
        ),
        out_specs=(
            P(None, "ctx", "head"),
            P("head", None, None),
            P("head", None, None),
            P("head", None, None),
        ),
        check_vma=False,
    )
```
